256 devices in a mesh: section: 8 (over z_lo, core), expert: 32 (over y, z_hi, x).
Axes of the slice: x: 4, y: 4, z: 8 (z_hi: 2, z_lo: 4; z = z_hi * 4 + z_lo), core: 2. Of those that a mesh axis runs over, the one named last changes fastest.
Arguments:
- x_held: bfloat16 [8, 4096, 2048], P('section', 'expert'), may hold values from -6 to 6
- grad_held: bfloat16 [8, 4096, 2048], P('section', 'expert'), may hold values from -6 to 6
- expert_ids: int32 [8, 4096, 4], P('section', 'expert'), may hold values from 0 to 27, all different within a row; in each aligned block of 128 rows (0 to 127, 128 to 255, ..., all dimensions but the last counted through in order) at most 23 rows name the same one
- gate_logits: float32 [8, 4096, 4], P('section', 'expert'), may hold values from -4 to 4
- placement: int32 [8, 32], P('section'), may hold values from 0 to 27, as said below
- w_gate_up: bfloat16 [8, 32, 2048, 1536], P('section', 'expert'), as said below
- w_down: bfloat16 [8, 32, 768, 2048], P('section', 'expert'), as said below
Outputs:
- section_out: bfloat16 [8, 4096, 2048], P('section', 'expert')
- input_grad: bfloat16 [8, 4096, 2048], P('section', 'expert')
- logit_grad: float32 [8, 4096, 4], P('section', 'expert')
The draws below stay inside these ranges and needn't reach their ends.
Inputs may be any that keep to these rules, and one draw needn't show every extreme that they name: `expert_ids`: in each section and the 128 tokens of one device, no expert is named by more than 23 slots, a bound that some such block reaches; a token names 4 different experts. `placement`: in each section, copies 0 to 27 hold every expert once, and copies 28 to 31 hold 4 different experts, a second copy each. `w_gate_up`: two copies of one section that hold the same expert have equal weights. `w_down`: two copies of one section that hold the same expert have equal weights.
All inputs are finite; a program needn't handle non-finite values.
Results may differ from the reference program's by a relative error of at most 0.0064.
Values may be sent and summed in bfloat16 or wider, within the bound.
No kernel may reach another device: no remote copies, remote signals or barrier semaphores. Data moves between devices by JAX's collectives and lax.ppermute only.
A program may use at most 128 MiB of HBM per device.

```python
import math
import jax
import jax.numpy as jnp
import numpy as np
from jax import lax

D = 2048
FF = 768
TOPK = 4
TOK_DEV = 128
COPIES = 32
REPL = 4
EXPERTS = 28
MOST = 23
TOKENS = 4096
N_SECTION = 8
N_EXPERT = 32


def section_tables(key):

    def one_section(section):
        section_key = jax.random.fold_in(key, section)
        base = jax.random.permutation(jax.random.fold_in(section_key, 1), EXPERTS)
        extra = jax.random.permutation(jax.random.fold_in(section_key, 2), EXPERTS)[:REPL]
        return jnp.concatenate([base, extra]).astype(jnp.int32)
    return jax.vmap(one_section)(jnp.arange(N_SECTION, dtype=jnp.int32))


def expert_keys(key, tables):

    def one_key(section, expert):
        return jax.random.fold_in(jax.random.fold_in(key, section), expert)
    sections = jnp.broadcast_to(jnp.arange(N_SECTION, dtype=jnp.int32)[:, None], tables.shape)
    return jax.vmap(jax.vmap(one_key))(sections, tables)


def draw_placement(key, part):
    return section_tables(key)


def draw_w_gate_up(key, part):
    tables = section_tables(key)
    key = jax.random.fold_in(key, 11)
    keys = expert_keys(key, tables)
    values = jax.vmap(jax.vmap(lambda single_key: jax.random.normal(single_key, (D, 2 * FF), jnp.float32)))(keys)
    return (values * D ** (-0.5)).astype(jnp.bfloat16)


def draw_w_down(key, part):
    tables = section_tables(key)
    key = jax.random.fold_in(key, 13)
    keys = expert_keys(key, tables)
    values = jax.vmap(jax.vmap(lambda single_key: jax.random.normal(single_key, (FF, D), jnp.float32)))(keys)
    return (values * FF ** (-0.5)).astype(jnp.bfloat16)


def level_of(stream_key, extent, split, smallest, largest):
    def one(dim, shards_of):
        draws = jax.random.uniform(jax.random.fold_in(jax.random.fold_in(stream_key, 6), dim), (shards_of,), jnp.float32, smallest / len(split), largest / len(split))
        return jnp.repeat(jnp.exp(draws), extent[dim] // shards_of).reshape((-1,) + (1,) * (len(extent) - dim - 1))

    gain = one(*split[0])
    for cut in split[1:]:
        gain = gain * one(*cut)
    return gain


def routed_block(key, own, number, rows, count, top, limit, skew):
    order = jax.random.permutation(key, count)
    heavy_load, ordinary = shares(count, rows * top, limit, skew, True), shares(count, rows * top, limit, skew, False)
    places = jnp.arange(count)

    def named(tallies, turn):
        used = int((tallies > 0).sum())
        fixed = max(1, used // 4)
        passed = fixed + (places - fixed + turn * (used - fixed)) % max(1, count - fixed)
        return jnp.zeros((count,), jnp.int32).at[order[jnp.where(places < fixed, places, passed)]].set(jnp.asarray(tallies, jnp.int32))

    tallies = jnp.where(number % 4 == 0, named(heavy_load, number // 4), named(ordinary, number - number // 4 - 1))
    mixed = jax.random.permutation(jax.random.fold_in(own, 3), count)
    donor, taker = mixed[0:count // 2 * 2:2], mixed[1:count // 2 * 2:2]
    room = jnp.minimum(tallies[donor] - 1, limit - tallies[taker]) // 2
    room = jnp.where((donor == order[0]) | (taker == order[0]) | (tallies[taker] == 0), 0, jnp.maximum(room, 0))
    passed = jax.random.randint(jax.random.fold_in(own, 4), (count // 2,), 0, 1 << 20) % (room + 1)
    tallies = tallies.at[donor].add(-passed).at[taker].add(passed)
    items = jnp.searchsorted(jnp.cumsum(tallies), jnp.arange(rows * top), side="right").astype(jnp.int32)
    listing = items.reshape(top, rows).T
    listing = listing[jax.random.permutation(jax.random.fold_in(own, 1), rows)]
    turn = jax.random.randint(jax.random.fold_in(own, 2), (rows, 1), 0, top)
    return jnp.take_along_axis(listing, (jnp.arange(top)[None, :] + turn) % top, axis=1)


def shares(amount, total, limit, skew, full):
    portions = [(1 << 20) // math.isqrt(grade ** skew) + 1 for grade in range(1, amount + 1)]
    largest = limit if full else min(limit, max(-(-total // amount), total * portions[0] // sum(portions)))
    least = 1 if total - largest >= amount - 1 else 0
    given, surplus = [largest] + [least] * (amount - 1), total - largest - least * (amount - 1)
    while surplus > 0:
        candidates = [i for i in range(1, amount) if given[i] < largest] or [i for i in range(1, amount) if given[i] < limit]
        mass, left = sum([portions[i] for i in candidates]), surplus
        for i in candidates:
            addition = min(limit - given[i], max(1, left * portions[i] // mass), surplus)
            given[i] = given[i] + addition
            surplus = surplus - addition
    return np.array(given)


def noise(key, shape, scale, limit, pieces=(), held_as=jnp.bfloat16):
    level = level_of(key, shape, pieces, -0.22, 0.18) if pieces else 1.0
    result = jax.random.normal(key, shape, jnp.float32) * scale * level
    return jnp.minimum(jnp.maximum(result, -limit), limit).astype(held_as)


def setup_inputs(seed: int = 0) -> dict:
    key_of = jax.random.split(jax.random.key(seed), 8)
    x_held = noise(key_of[0], (N_SECTION, TOKENS, D), 1.0, 6.0, ((0, 8), (1, 32)))
    grad_held = noise(key_of[1], (N_SECTION, TOKENS, D), 1.0, 6.0, ((0, 8), (1, 32)))
    expert_ids_keys = jax.random.split(jax.random.fold_in(key_of[2], 1), N_SECTION * TOKENS // TOK_DEV)
    expert_ids_turns = jax.random.permutation(jax.random.fold_in(key_of[2], 3), N_SECTION * TOKENS // TOK_DEV)
    expert_ids = jax.vmap(lambda own, number: routed_block(jax.random.fold_in(key_of[2], 2), own, number, TOK_DEV, EXPERTS, TOPK, MOST, 2))(expert_ids_keys, expert_ids_turns).reshape((N_SECTION, TOKENS, TOPK))
    gate_logits = noise(key_of[3], (N_SECTION, TOKENS, TOPK), 1.0, 4.0, ((0, 8), (1, 32)), jnp.float32)
    placement = draw_placement(jax.random.fold_in(key_of[7], 71), 0)
    w_gate_up = draw_w_gate_up(jax.random.fold_in(key_of[7], 71), 0)
    w_down = draw_w_down(jax.random.fold_in(key_of[7], 71), 0)
    return {"x_held": x_held, "grad_held": grad_held, "expert_ids": expert_ids, "gate_logits": gate_logits, "placement": placement, "w_gate_up": w_gate_up, "w_down": w_down}


def routing(expert_list, table):
    flat_ids = expert_list.reshape(-1)
    labels = jnp.arange(EXPERTS, dtype=jnp.int32)
    onehot = (flat_ids[:, None] == labels[None, :]).astype(jnp.int32)
    before = jnp.cumsum(onehot, axis=0) - onehot
    ranking = jnp.sum(before * onehot, axis=1)
    holding = (table[:, None] == labels[None, :]).astype(jnp.int32)
    number = jnp.arange(COPIES, dtype=jnp.int32)[:, None]
    first_mask = (number < EXPERTS).astype(jnp.int32)
    primary = jnp.sum(number * holding * first_mask, axis=0)
    second = jnp.sum(number * holding * (1 - first_mask), axis=0)
    doubled = jnp.sum(holding * (1 - first_mask), axis=0)
    to_first = jnp.sum(onehot * primary[None, :], axis=1)
    to_second = jnp.sum(onehot * second[None, :], axis=1)
    is_hot = jnp.sum(onehot * doubled[None, :], axis=1)
    target = jnp.where((is_hot > 0) & (ranking % 2 == 1), to_second, to_first)
    marked = (target[:, None] == jnp.arange(COPIES, dtype=jnp.int32)[None, :]).astype(jnp.int32)
    places = jnp.sum((jnp.cumsum(marked, axis=0) - marked) * marked, axis=1)
    return target, places


def slot_index(target, places):
    total = target.shape[0]
    empty = jnp.full((COPIES * MOST,), total, dtype=jnp.int32)
    return empty.at[target * MOST + places].set(jnp.arange(total, dtype=jnp.int32))


def pick_rows(source, index):
    padded = jnp.concatenate([source, jnp.zeros((1, source.shape[1]), source.dtype)], axis=0)
    return jnp.take(padded, index, axis=0)


def expert_pair(packed):
    rows, grads, w_gu, w_dn = packed
    pre_acts = jnp.dot(rows, w_gu, preferred_element_type=jnp.float32)
    gate_pre = pre_acts[:, :FF]
    up_pre = pre_acts[:, FF:]
    sigmoid_gate = jax.nn.sigmoid(gate_pre)
    hidden = (gate_pre * sigmoid_gate * up_pre).astype(jnp.bfloat16)
    produced = jnp.dot(hidden, w_dn, preferred_element_type=jnp.float32).astype(jnp.bfloat16)
    hidden_grad = jnp.dot(grads, w_dn.T, preferred_element_type=jnp.float32)
    pre_grad = jnp.concatenate([hidden_grad * up_pre * sigmoid_gate * (1.0 + gate_pre * (1.0 - sigmoid_gate)), hidden_grad * gate_pre * sigmoid_gate], axis=1).astype(jnp.bfloat16)
    row_grad = jnp.dot(pre_grad, w_gu.T, preferred_element_type=jnp.float32).astype(jnp.bfloat16)
    return produced, row_grad


def one_section(packed):
    section_in, section_grad, section_ids, section_logits, table, w_gu, w_dn = packed
    sources = section_in.reshape(N_EXPERT, TOK_DEV, D)
    grads = section_grad.reshape(N_EXPERT, TOK_DEV, D)
    logits = section_logits.reshape(N_EXPERT, TOK_DEV, TOPK)
    raised = jnp.exp(logits)
    gate_probs = raised / jnp.sum(raised, axis=2, keepdims=True)
    targets, places = jax.vmap(routing, in_axes=(0, None))(section_ids.reshape(N_EXPERT, TOK_DEV, TOPK), table)
    total = TOK_DEV * TOPK
    index = jax.vmap(slot_index)(targets, places)
    token_of = jnp.where(index < total, index // TOPK, TOK_DEV).astype(jnp.int32)
    rows = jax.vmap(pick_rows)(sources, token_of)
    scaled = (gate_probs[:, :, :, None] * grads[:, :, None, :].astype(jnp.float32)).astype(jnp.bfloat16)
    grad_rows = jax.vmap(pick_rows)(scaled.reshape(N_EXPERT, total, D), index)
    copy_rows = rows.reshape(N_EXPERT, COPIES, MOST, D).transpose(1, 0, 2, 3).reshape(COPIES, N_EXPERT * MOST, D)
    copy_grads = grad_rows.reshape(N_EXPERT, COPIES, MOST, D).transpose(1, 0, 2, 3).reshape(COPIES, N_EXPERT * MOST, D)
    produced, row_grad = lax.map(expert_pair, (copy_rows, copy_grads, w_gu, w_dn))
    produced = produced.reshape(COPIES, N_EXPERT, MOST, D).transpose(1, 0, 2, 3).reshape(N_EXPERT, COPIES * MOST, D)
    row_grad = row_grad.reshape(COPIES, N_EXPERT, MOST, D).transpose(1, 0, 2, 3).reshape(N_EXPERT, COPIES * MOST, D)
    where_from = (targets * MOST + places).astype(jnp.int32)
    take_rows = jax.vmap(lambda whole, spots: jnp.take(whole, spots, axis=0))
    out_slots = take_rows(produced, where_from).reshape(N_EXPERT, TOK_DEV, TOPK, D)
    grad_slots = take_rows(row_grad, where_from).reshape(N_EXPERT, TOK_DEV, TOPK, D)
    section_out = jnp.sum(gate_probs[:, :, :, None] * out_slots.astype(jnp.float32), axis=2).astype(jnp.bfloat16)
    gate_grad = jnp.einsum("stkd,std->stk", out_slots.astype(jnp.float32), grads.astype(jnp.float32))
    logit_grad = gate_probs * (gate_grad - jnp.sum(gate_probs * gate_grad, axis=2, keepdims=True))
    input_grad = jnp.sum(grad_slots.astype(jnp.float32), axis=2).astype(jnp.bfloat16)
    return section_out.reshape(TOKENS, D), input_grad.reshape(TOKENS, D), logit_grad.reshape(TOKENS, TOPK)


def reference(x_held, grad_held, expert_ids, gate_logits, placement, w_gate_up, w_down):
    inputs = jnp.concatenate([x_held[:1], x_held[:-1]], axis=0)
    upstream = jnp.concatenate([grad_held[1:], grad_held[-1:]], axis=0)
    section_out, input_grad, logit_grad = lax.map(one_section, (inputs, upstream, expert_ids, gate_logits, placement, w_gate_up, w_down))
    return (section_out, input_grad, logit_grad)
```

```python
import functools

import jax
import jax.numpy as jnp
from jax import lax
from jax.experimental import pallas as pl
from jax.experimental.pallas import tpu as pltpu
from jax.sharding import Mesh, PartitionSpec as P

F32 = jnp.float32
BF16 = jnp.bfloat16
SECTION = ("z_lo", "core")
EXPERT = ("y", "z_hi", "x")
PLANE = ("y", "x")
SIZES = (4, 2, 4, 2, 4)
CAP = 24
VMEM_BYTES = 48 * 1024 * 1024
ANYWHERE = pl.BlockSpec(memory_space=pltpu.VMEM)
SCALAR = pl.BlockSpec(memory_space=pltpu.SMEM)


def dot(a, b, ca, cb):
    return lax.dot_general(a, b, (((ca,), (cb,)), ((), ())), preferred_element_type=F32)


def probabilities(meta):
    raised = jnp.exp(meta[4:8, :])
    return raised / jnp.sum(raised, axis=0, keepdims=True)


def row_marks(meta, table, half, rows):
    copies = table.shape[1]
    tokens = meta.shape[1]
    experts = copies - copies // 8
    ids = meta[0:4, :].astype(jnp.int32)
    label = lax.broadcasted_iota(jnp.int32, (copies, tokens), 0)
    named = [ids[k : k + 1, :] == label for k in range(4)]
    onehot = sum(n.astype(F32) for n in named).astype(BF16)
    earlier = (
        lax.broadcasted_iota(jnp.int32, (tokens, tokens), 0)
        < lax.broadcasted_iota(jnp.int32, (tokens, tokens), 1)
    ).astype(F32).astype(BF16)
    rank = dot(onehot, earlier, 1, 0).astype(jnp.int32)
    copy = lax.broadcasted_iota(jnp.int32, (copies, copies), 1)
    held = table == lax.broadcasted_iota(jnp.int32, (copies, copies), 0)
    first = jnp.sum(jnp.where(held & (copy < experts), copy, 0), axis=1, keepdims=True)
    second = jnp.sum(jnp.where(held & (copy >= experts), copy, 0), axis=1, keepdims=True)
    hot = second > 0
    target = jnp.where(hot & ((rank & 1) == 1), second, first)
    place = jnp.where(hot, rank >> 1, rank)
    row = ((target >> 3) * 4 + (target & 3)) * CAP + place
    row = jnp.where(((target >> 2) & 1) == half, row, -1)
    number = lax.broadcasted_iota(jnp.int32, (rows, tokens), 0)
    return [
        number == jnp.sum(jnp.where(n, row, 0), axis=0, keepdims=True) for n in named
    ]


def either(marks):
    return sum(m.astype(F32) for m in marks)


def weighted(marks, probs):
    return sum(jnp.where(m, probs[k : k + 1, :], 0.0) for k, m in enumerate(marks))


def pack_kernel(half_ref, meta_ref, table_ref, x_ref, out_ref, *, scaled):
    meta = meta_ref[...]
    marks = row_marks(meta, table_ref[...], half_ref[0], out_ref.shape[0])
    picked = dot(either(marks).astype(BF16), x_ref[...], 1, 0)
    if scaled:
        weight = jnp.sum(weighted(marks, probabilities(meta)), axis=1, keepdims=True)
        picked = picked * weight
    out_ref[...] = picked.astype(BF16)


def pack(half, meta, table, x, scaled):
    rows = 16 * CAP
    return pl.pallas_call(
        functools.partial(pack_kernel, scaled=scaled),
        out_shape=jax.ShapeDtypeStruct((rows, x.shape[1]), BF16),
        in_specs=[SCALAR, ANYWHERE, ANYWHERE, ANYWHERE],
        out_specs=ANYWHERE,
        compiler_params=pltpu.CompilerParams(vmem_limit_bytes=VMEM_BYTES),
        cost_estimate=pl.CostEstimate(
            flops=2 * rows * x.size, bytes_accessed=2 * x.size + 2 * rows * x.shape[1], transcendentals=0
        ),
        name="pack_grad" if scaled else "pack_in",
    )(half, meta, table, x)


def split_dot(weights, rows):
    high = weights.astype(BF16)
    low = (weights - high.astype(F32)).astype(BF16)
    return dot(high, rows, 0, 0) + dot(low, rows, 0, 0)


def out_kernel(half_ref, meta_ref, table_ref, rows_ref, g_ref, *refs, last):
    meta = meta_ref[...]
    rows = rows_ref[...]
    marks = row_marks(meta, table_ref[...], half_ref[0], rows.shape[0])
    probs = probabilities(meta)
    total = split_dot(weighted(marks, probs), rows)
    products = dot(rows, g_ref[...], 1, 1)
    grads = jnp.concatenate(
        [jnp.sum(jnp.where(m, products, 0.0), axis=0, keepdims=True) for m in marks], axis=0
    )
    if last:
        other_ref, other_grads_ref, out_ref, logit_ref = refs
        out_ref[...] = (total + other_ref[...].astype(F32)).astype(BF16)
        grads = grads + other_grads_ref[0:4, :]
        logit_ref[...] = probs * (grads - jnp.sum(probs * grads, axis=0, keepdims=True))
    else:
        out_ref, grads_ref = refs
        out_ref[...] = total.astype(BF16)
        grads_ref[...] = jnp.concatenate([grads, jnp.zeros_like(grads)], axis=0)


def collect_out(half, meta, table, rows, g, other=None):
    last = other is not None
    extra = list(other) if last else []
    return pl.pallas_call(
        functools.partial(out_kernel, last=last),
        out_shape=(
            jax.ShapeDtypeStruct(g.shape, BF16),
            jax.ShapeDtypeStruct((4 if last else 8, g.shape[0]), F32),
        ),
        in_specs=[SCALAR] + [ANYWHERE] * (4 + len(extra)),
        out_specs=(ANYWHERE, ANYWHERE),
        compiler_params=pltpu.CompilerParams(vmem_limit_bytes=VMEM_BYTES),
        cost_estimate=pl.CostEstimate(
            flops=6 * rows.shape[0] * g.size, bytes_accessed=2 * rows.size + 4 * g.size, transcendentals=0
        ),
        name="collect_out_last" if last else "collect_out",
    )(half, meta, table, rows, g, *extra)


def grad_kernel(half_ref, meta_ref, table_ref, rows_ref, *refs, last):
    rows = rows_ref[...]
    marks = row_marks(meta_ref[...], table_ref[...], half_ref[0], rows.shape[0])
    total = dot(either(marks).astype(BF16), rows, 0, 0)
    if last:
        total = total + refs[0][...].astype(F32)
    refs[-1][...] = total.astype(BF16)


def collect_grad(half, meta, table, rows, other=None):
    last = other is not None
    extra = [other] if last else []
    tokens = meta.shape[1]
    return pl.pallas_call(
        functools.partial(grad_kernel, last=last),
        out_shape=jax.ShapeDtypeStruct((tokens, rows.shape[1]), BF16),
        in_specs=[SCALAR] + [ANYWHERE] * (3 + len(extra)),
        out_specs=ANYWHERE,
        compiler_params=pltpu.CompilerParams(vmem_limit_bytes=VMEM_BYTES),
        cost_estimate=pl.CostEstimate(
            flops=2 * rows.size * tokens, bytes_accessed=2 * rows.size + 2 * tokens * rows.shape[1], transcendentals=0
        ),
        name="collect_grad_last" if last else "collect_grad",
    )(half, meta, table, rows, *extra)


def forward_kernel(x_ref, wg_ref, wu_ref, wd_ref, out_ref, gate_ref, up_ref, total):
    step = pl.program_id(0)
    x = x_ref[...]
    gate = dot(x, wg_ref[...], 1, 0)
    up = dot(x, wu_ref[...], 1, 0)
    gate_ref[...] = gate
    up_ref[...] = up
    hidden = (gate * jax.nn.sigmoid(gate) * up).astype(BF16)
    part = dot(hidden, wd_ref[...], 1, 0)

    @pl.when(step == 0)
    def _():
        total[...] = part

    @pl.when(step > 0)
    def _():
        total[...] += part

    @pl.when(step == pl.num_programs(0) - 1)
    def _():
        out_ref[...] = total[...].astype(BF16)


def backward_kernel(g_ref, gate_ref, up_ref, wg_ref, wu_ref, wd_ref, out_ref, total):
    step = pl.program_id(0)
    hidden_grad = dot(g_ref[...], wd_ref[...], 1, 1)
    gate = gate_ref[...]
    up = up_ref[...]
    sigmoid = jax.nn.sigmoid(gate)
    gate_grad = (hidden_grad * up * sigmoid * (1.0 + gate * (1.0 - sigmoid))).astype(BF16)
    up_grad = (hidden_grad * gate * sigmoid).astype(BF16)
    part = dot(gate_grad, wg_ref[...], 1, 1) + dot(up_grad, wu_ref[...], 1, 1)

    @pl.when(step == 0)
    def _():
        total[...] = part

    @pl.when(step > 0)
    def _():
        total[...] += part

    @pl.when(step == pl.num_programs(0) - 1)
    def _():
        out_ref[...] = total[...].astype(BF16)


BLOCK = 256


def expert_specs(rows, width, hidden):
    steps = hidden // BLOCK
    whole = pl.BlockSpec((rows, width), lambda j: (0, 0))
    gate = pl.BlockSpec((width, BLOCK), lambda j: (0, j))
    up = pl.BlockSpec((width, BLOCK), lambda j: (0, steps + j))
    down = pl.BlockSpec((BLOCK, width), lambda j: (j, 0))
    pre = pl.BlockSpec((rows, BLOCK), lambda j: (0, j))
    return steps, whole, gate, up, down, pre


def expert_cost(rows, width, hidden):
    return pl.CostEstimate(
        flops=6 * rows * width * hidden,
        bytes_accessed=6 * width * hidden + 4 * rows * width + 8 * rows * hidden,
        transcendentals=rows * hidden,
    )


def expert_forward(x, w_gu, w_dn):
    rows, width = x.shape
    hidden = w_dn.shape[0]
    steps, whole, gate, up, down, pre = expert_specs(rows, width, hidden)
    return pl.pallas_call(
        forward_kernel,
        grid=(steps,),
        out_shape=(
            jax.ShapeDtypeStruct((rows, width), BF16),
            jax.ShapeDtypeStruct((rows, hidden), F32),
            jax.ShapeDtypeStruct((rows, hidden), F32),
        ),
        in_specs=[whole, gate, up, down],
        out_specs=(whole, pre, pre),
        scratch_shapes=[pltpu.VMEM((rows, width), F32)],
        compiler_params=pltpu.CompilerParams(vmem_limit_bytes=VMEM_BYTES),
        cost_estimate=expert_cost(rows, width, hidden),
        name="expert_forward",
    )(x, w_gu, w_gu, w_dn)


def expert_backward(g, gates, ups, w_gu, w_dn):
    rows, width = g.shape
    hidden = w_dn.shape[0]
    steps, whole, gate, up, down, pre = expert_specs(rows, width, hidden)
    return pl.pallas_call(
        backward_kernel,
        grid=(steps,),
        out_shape=jax.ShapeDtypeStruct((rows, width), BF16),
        in_specs=[whole, pre, pre, gate, up, down],
        out_specs=whole,
        scratch_shapes=[pltpu.VMEM((rows, width), F32)],
        compiler_params=pltpu.CompilerParams(vmem_limit_bytes=VMEM_BYTES),
        cost_estimate=expert_cost(rows, width, hidden),
        name="expert_backward",
    )(g, gates, ups, w_gu, w_gu, w_dn)


def passed_along(x, by):
    devices = SIZES[0] * SIZES[1]
    pairs = [(i, i + by) for i in range(devices) if 0 <= i + by < devices]
    return lax.ppermute(x, SECTION, pairs)


def swapped(x):
    return lax.ppermute(x, "z_hi", [(0, 1), (1, 0)])


def exchanged(rows):
    width = rows.shape[-1]
    moved = lax.all_to_all(
        rows.reshape(16, CAP, width), PLANE, split_axis=0, concat_axis=0, tiled=True
    )
    return moved.reshape(16 * CAP, width)


def local(x_held, grad_held, expert_ids, gate_logits, placement, w_gate_up, w_down):
    own_x = x_held[0]
    own_g = grad_held[0]
    w_gu = w_gate_up[0, 0]
    w_dn = w_down[0, 0]
    section = lax.axis_index(SECTION)
    sections = SIZES[0] * SIZES[1]
    half = lax.axis_index("z_hi").astype(jnp.int32).reshape(1)
    table = placement

    meta = jnp.concatenate([expert_ids[0].astype(F32).T, gate_logits[0].T], axis=0)
    meta_other = swapped(meta)
    x = jnp.where(section == 0, own_x, passed_along(own_x, 1))
    g = jnp.where(section == sections - 1, own_g, passed_along(own_g, -1))
    x_other = swapped(x)
    g_other = swapped(g)

    x_rows = exchanged(pack(half, meta, table, x, False))
    x_rows_other = exchanged(pack(half, meta_other, table, x_other, False))
    g_rows = exchanged(pack(half, meta, table, g, True))
    g_rows_other = exchanged(pack(half, meta_other, table, g_other, True))

    out, gate, up = expert_forward(x_rows, w_gu, w_dn)
    out_other, gate_other, up_other = expert_forward(x_rows_other, w_gu, w_dn)
    out_other = exchanged(out_other)
    out = exchanged(out)
    back_other = exchanged(expert_backward(g_rows_other, gate_other, up_other, w_gu, w_dn))
    back = exchanged(expert_backward(g_rows, gate, up, w_gu, w_dn))

    part, part_grads = collect_out(half, meta_other, table, out_other, g_other)
    part = swapped(part)
    part_grads = swapped(part_grads)
    back_part = swapped(collect_grad(half, meta_other, table, back_other))
    section_out, logit_grad = collect_out(half, meta, table, out, g, (part, part_grads))
    input_grad = collect_grad(half, meta, table, back, back_part)
    return section_out[None], input_grad[None], logit_grad.T[None]


def solution(mesh):
    fine = Mesh(mesh.devices.reshape(SIZES), SECTION + EXPERT)
    placed = (
        P(SECTION, EXPERT, None),
        P(SECTION, EXPERT, None),
        P(SECTION, EXPERT, None),
        P(SECTION, EXPERT, None),
        P(SECTION, None),
        P(SECTION, EXPERT, None, None),
        P(SECTION, EXPERT, None, None),
    )
    return jax.shard_map(
        local,
        mesh=fine,
        in_specs=placed,
        out_specs=(P(SECTION, EXPERT, None),) * 3,
        check_vma=False,
    )
```

```python
import functools

import jax
import jax.numpy as jnp
from jax import lax
from jax.experimental import pallas as pl
from jax.experimental.pallas import tpu as pltpu
from jax.sharding import Mesh, PartitionSpec as P

F32 = jnp.float32
BF16 = jnp.bfloat16
SECTION = ("z_lo", "core")
EXPERT = ("y", "z_hi", "x")
PLANE = ("y", "x")
SIZES = (4, 2, 4, 2, 4)
CAP = 24
VMEM_BYTES = 48 * 1024 * 1024
ANYWHERE = pl.BlockSpec(memory_space=pltpu.VMEM)
SCALAR = pl.BlockSpec(memory_space=pltpu.SMEM)


def dot(a, b, ca, cb):
    return lax.dot_general(a, b, (((ca,), (cb,)), ((), ())), preferred_element_type=F32)


def probabilities(meta):
    raised = jnp.exp(meta[4:8, :])
    return raised / jnp.sum(raised, axis=0, keepdims=True)


def row_marks(meta, table, half, rows, stride=CAP, offset=0):
    copies = table.shape[1]
    tokens = meta.shape[1]
    experts = copies - copies // 8
    ids = meta[0:4, :].astype(jnp.int32)
    label = lax.broadcasted_iota(jnp.int32, (copies, tokens), 0)
    named = [ids[k : k + 1, :] == label for k in range(4)]
    onehot = sum(n.astype(F32) for n in named).astype(BF16)
    earlier = (
        lax.broadcasted_iota(jnp.int32, (tokens, tokens), 0)
        < lax.broadcasted_iota(jnp.int32, (tokens, tokens), 1)
    ).astype(F32).astype(BF16)
    rank = dot(onehot, earlier, 1, 0).astype(jnp.int32)
    copy = lax.broadcasted_iota(jnp.int32, (copies, copies), 1)
    held = table == lax.broadcasted_iota(jnp.int32, (copies, copies), 0)
    first = jnp.sum(jnp.where(held & (copy < experts), copy, 0), axis=1, keepdims=True)
    second = jnp.sum(jnp.where(held & (copy >= experts), copy, 0), axis=1, keepdims=True)
    hot = second > 0
    target = jnp.where(hot & ((rank & 1) == 1), second, first)
    place = jnp.where(hot, rank >> 1, rank)
    row = ((target >> 3) * 4 + (target & 3)) * stride + offset + place
    row = jnp.where(((target >> 2) & 1) == half, row, -1)
    number = lax.broadcasted_iota(jnp.int32, (rows, tokens), 0)
    return [
        number == jnp.sum(jnp.where(n, row, 0), axis=0, keepdims=True) for n in named
    ]


def either(marks):
    return sum(m.astype(F32) for m in marks)


def weighted(marks, probs):
    return sum(jnp.where(m, probs[k : k + 1, :], 0.0) for k, m in enumerate(marks))


def both_marks(own, other, table, half, rows):
    return [
        row_marks(meta, table, half, rows, 2 * CAP, i * CAP) for i, meta in enumerate((own, other))
    ]


def pack_kernel(half_ref, meta_ref, meta_other_ref, table_ref, x_ref, x_other_ref, out_ref, *, scaled):
    metas = meta_ref[...], meta_other_ref[...]
    marks = both_marks(*metas, table_ref[...], half_ref[0], out_ref.shape[0])
    onehot = jnp.concatenate([either(m) for m in marks], axis=1).astype(BF16)
    picked = dot(onehot, jnp.concatenate([x_ref[...], x_other_ref[...]], axis=0), 1, 0)
    if scaled:
        probs = [weighted(m, probabilities(meta)) for m, meta in zip(marks, metas)]
        picked = picked * jnp.sum(probs[0] + probs[1], axis=1, keepdims=True)
    out_ref[...] = picked.astype(BF16)


def pack(half, meta, meta_other, table, x, x_other, scaled):
    rows = 32 * CAP
    return pl.pallas_call(
        functools.partial(pack_kernel, scaled=scaled),
        out_shape=jax.ShapeDtypeStruct((rows, x.shape[1]), BF16),
        in_specs=[SCALAR] + [ANYWHERE] * 5,
        out_specs=ANYWHERE,
        compiler_params=pltpu.CompilerParams(vmem_limit_bytes=VMEM_BYTES),
        cost_estimate=pl.CostEstimate(
            flops=4 * rows * x.size, bytes_accessed=4 * x.size + 2 * rows * x.shape[1], transcendentals=0
        ),
        name="pack_grad" if scaled else "pack_in",
    )(half, meta, meta_other, table, x, x_other)


def split_dot(weights, rows):
    high = weights.astype(BF16)
    low = (weights - high.astype(F32)).astype(BF16)
    return dot(high, rows, 0, 0) + dot(low, rows, 0, 0)


def out_kernel(
    half_ref, meta_ref, meta_other_ref, table_ref, rows_ref, g_ref, g_other_ref,
    own_ref, own_grads_ref, other_ref, other_grads_ref,
):
    metas = meta_ref[...], meta_other_ref[...]
    rows = rows_ref[...]
    marks = both_marks(*metas, table_ref[...], half_ref[0], rows.shape[0])
    weights = [weighted(m, probabilities(meta)) for m, meta in zip(marks, metas)]
    own_ref[...] = split_dot(weights[0], rows)
    other_ref[...] = split_dot(weights[1], rows).astype(BF16)
    for ref, m, grads in zip((own_grads_ref, other_grads_ref), marks, (g_ref, g_other_ref)):
        products = dot(rows, grads[...], 1, 1)
        sums = [jnp.sum(jnp.where(k, products, 0.0), axis=0, keepdims=True) for k in m]
        ref[...] = jnp.concatenate(sums + [jnp.zeros_like(s) for s in sums], axis=0)


def collect_out(half, meta, meta_other, table, rows, g, g_other):
    sums = jax.ShapeDtypeStruct((8, g.shape[0]), F32)
    return pl.pallas_call(
        out_kernel,
        out_shape=(
            jax.ShapeDtypeStruct(g.shape, F32),
            sums,
            jax.ShapeDtypeStruct(g.shape, BF16),
            sums,
        ),
        in_specs=[SCALAR] + [ANYWHERE] * 6,
        out_specs=(ANYWHERE,) * 4,
        compiler_params=pltpu.CompilerParams(vmem_limit_bytes=VMEM_BYTES),
        cost_estimate=pl.CostEstimate(
            flops=12 * rows.shape[0] * g.size, bytes_accessed=2 * rows.size + 12 * g.size, transcendentals=0
        ),
        name="collect_out",
    )(half, meta, meta_other, table, rows, g, g_other)


def finish_kernel(meta_ref, own_ref, own_grads_ref, other_ref, other_grads_ref, out_ref, logit_ref):
    out_ref[...] = (own_ref[...] + other_ref[...].astype(F32)).astype(BF16)
    probs = probabilities(meta_ref[...])
    grads = own_grads_ref[0:4, :] + other_grads_ref[0:4, :]
    logit_ref[...] = probs * (grads - jnp.sum(probs * grads, axis=0, keepdims=True))


def finish_out(meta, own, own_grads, other, other_grads):
    return pl.pallas_call(
        finish_kernel,
        out_shape=(
            jax.ShapeDtypeStruct(own.shape, BF16),
            jax.ShapeDtypeStruct((4, own.shape[0]), F32),
        ),
        in_specs=[ANYWHERE] * 5,
        out_specs=(ANYWHERE, ANYWHERE),
        compiler_params=pltpu.CompilerParams(vmem_limit_bytes=VMEM_BYTES),
        cost_estimate=pl.CostEstimate(flops=2 * own.size, bytes_accessed=8 * own.size, transcendentals=0),
        name="finish_out",
    )(meta, own, own_grads, other, other_grads)


def grad_kernel(half_ref, meta_ref, table_ref, rows_ref, *refs, last):
    rows = rows_ref[...]
    marks = row_marks(meta_ref[...], table_ref[...], half_ref[0], rows.shape[0])
    total = dot(either(marks).astype(BF16), rows, 0, 0)
    if last:
        total = total + refs[0][...].astype(F32)
    refs[-1][...] = total.astype(BF16)


def collect_grad(half, meta, table, rows, other=None):
    last = other is not None
    extra = [other] if last else []
    tokens = meta.shape[1]
    return pl.pallas_call(
        functools.partial(grad_kernel, last=last),
        out_shape=jax.ShapeDtypeStruct((tokens, rows.shape[1]), BF16),
        in_specs=[SCALAR] + [ANYWHERE] * (3 + len(extra)),
        out_specs=ANYWHERE,
        compiler_params=pltpu.CompilerParams(vmem_limit_bytes=VMEM_BYTES),
        cost_estimate=pl.CostEstimate(
            flops=2 * rows.size * tokens, bytes_accessed=2 * rows.size + 2 * tokens * rows.shape[1], transcendentals=0
        ),
        name="collect_grad_last" if last else "collect_grad",
    )(half, meta, table, rows, *extra)


def forward_kernel(x_ref, wg_ref, wu_ref, wd_ref, out_ref, gate_ref, up_ref, total):
    step = pl.program_id(0)
    x = x_ref[...]
    gate = dot(x, wg_ref[...], 1, 0)
    up = dot(x, wu_ref[...], 1, 0)
    gate_ref[...] = gate
    up_ref[...] = up
    hidden = (gate * jax.nn.sigmoid(gate) * up).astype(BF16)
    part = dot(hidden, wd_ref[...], 1, 0)

    @pl.when(step == 0)
    def _():
        total[...] = part

    @pl.when(step > 0)
    def _():
        total[...] += part

    @pl.when(step == pl.num_programs(0) - 1)
    def _():
        out_ref[...] = total[...].astype(BF16)


def backward_kernel(g_ref, gate_ref, up_ref, wg_ref, wu_ref, wd_ref, own_ref, other_ref, total):
    step = pl.program_id(0)
    hidden_grad = dot(g_ref[...], wd_ref[...], 1, 1)
    gate = gate_ref[...]
    up = up_ref[...]
    sigmoid = jax.nn.sigmoid(gate)
    gate_grad = (hidden_grad * up * sigmoid * (1.0 + gate * (1.0 - sigmoid))).astype(BF16)
    up_grad = (hidden_grad * gate * sigmoid).astype(BF16)
    part = dot(gate_grad, wg_ref[...], 1, 1) + dot(up_grad, wu_ref[...], 1, 1)

    @pl.when(step == 0)
    def _():
        total[...] = part

    @pl.when(step > 0)
    def _():
        total[...] += part

    @pl.when(step == pl.num_programs(0) - 1)
    def _():
        for i in range(own_ref.shape[0]):
            own_ref[i] = total[2 * CAP * i : 2 * CAP * i + CAP, :].astype(BF16)
            other_ref[i] = total[2 * CAP * i + CAP : 2 * CAP * (i + 1), :].astype(BF16)


BLOCK = 256


def expert_specs(rows, width, hidden):
    steps = hidden // BLOCK
    whole = pl.BlockSpec((rows, width), lambda j: (0, 0))
    gate = pl.BlockSpec((width, BLOCK), lambda j: (0, j))
    up = pl.BlockSpec((width, BLOCK), lambda j: (0, steps + j))
    down = pl.BlockSpec((BLOCK, width), lambda j: (j, 0))
    pre = pl.BlockSpec((rows, BLOCK), lambda j: (0, j))
    return steps, whole, gate, up, down, pre


def expert_cost(rows, width, hidden):
    return pl.CostEstimate(
        flops=6 * rows * width * hidden,
        bytes_accessed=6 * width * hidden + 4 * rows * width + 8 * rows * hidden,
        transcendentals=rows * hidden,
    )


def expert_forward(x, w_gu, w_dn):
    rows, width = x.shape
    hidden = w_dn.shape[0]
    steps, whole, gate, up, down, pre = expert_specs(rows, width, hidden)
    return pl.pallas_call(
        forward_kernel,
        grid=(steps,),
        out_shape=(
            jax.ShapeDtypeStruct((rows, width), BF16),
            jax.ShapeDtypeStruct((rows, hidden), F32),
            jax.ShapeDtypeStruct((rows, hidden), F32),
        ),
        in_specs=[whole, gate, up, down],
        out_specs=(whole, pre, pre),
        scratch_shapes=[pltpu.VMEM((rows, width), F32)],
        compiler_params=pltpu.CompilerParams(vmem_limit_bytes=VMEM_BYTES),
        cost_estimate=expert_cost(rows, width, hidden),
        name="expert_forward",
    )(x, w_gu, w_gu, w_dn)


def expert_backward(g, gates, ups, w_gu, w_dn):
    rows, width = g.shape
    hidden = w_dn.shape[0]
    steps, whole, gate, up, down, pre = expert_specs(rows, width, hidden)
    block = (rows // (2 * CAP), CAP, width)
    return pl.pallas_call(
        backward_kernel,
        grid=(steps,),
        out_shape=(jax.ShapeDtypeStruct(block, BF16),) * 2,
        in_specs=[whole, pre, pre, gate, up, down],
        out_specs=(pl.BlockSpec(block, lambda j: (0, 0, 0)),) * 2,
        scratch_shapes=[pltpu.VMEM((rows, width), F32)],
        compiler_params=pltpu.CompilerParams(vmem_limit_bytes=VMEM_BYTES),
        cost_estimate=expert_cost(rows, width, hidden),
        name="expert_backward",
    )(g, gates, ups, w_gu, w_gu, w_dn)


def after(x, *earlier):
    return lax.optimization_barrier((x, *earlier))[0]


def shifted(x, by):
    sections = SIZES[0] * SIZES[1]
    pairs = [(i, i + by) for i in range(sections) if 0 <= i + by < sections]
    here = lax.axis_index(SECTION) == (0 if by > 0 else sections - 1)
    return jnp.where(here, x, lax.ppermute(x, SECTION, pairs))


def swapped(x, cores=(0, 1)):
    pairs = [(2 * c + h, 2 * c + 1 - h) for c in cores for h in range(2)]
    return lax.ppermute(x, ("core", "z_hi"), pairs)


def exchanged(rows):
    width = rows.shape[-1]
    moved = lax.all_to_all(
        rows.reshape(16, -1, width), PLANE, split_axis=0, concat_axis=0, tiled=True
    )
    return moved.reshape(-1, width)


def local(x_held, grad_held, expert_ids, gate_logits, placement, w_gate_up, w_down):
    w_gu = w_gate_up[0, 0]
    w_dn = w_down[0, 0]
    half = lax.axis_index("z_hi").astype(jnp.int32).reshape(1)
    table = placement

    meta = jnp.concatenate([expert_ids[0].astype(F32).T, gate_logits[0].T], axis=0)
    meta_other = swapped(meta)
    odd = lax.axis_index("core") == 1
    x_odd = lax.ppermute(
        x_held[0],
        SECTION + ("z_hi",),
        [(4 * i + h, 4 * i + 3 - h) for i in range(SIZES[0]) for h in range(2)],
    )
    x = shifted(x_held[0], 1)
    g = shifted(grad_held[0], -1)
    x_even = swapped(after(x, g), (0,))
    x_other = jnp.where(odd, x_odd, x_even)
    packed = pack(half, meta, meta_other, table, x, x_other, False)
    x_rows = exchanged(packed)
    g_other = swapped(after(g, packed))
    g_rows = exchanged(after(pack(half, meta, meta_other, table, g, g_other, True), x_rows))
    out, gate, up = expert_forward(x_rows, w_gu, w_dn)
    out = exchanged(after(out, g_rows))
    back, back_other = expert_backward(g_rows, gate, up, w_gu, w_dn)
    back_other = exchanged(after(back_other, out))

    own, own_grads, other, other_grads = collect_out(half, meta, meta_other, table, out, g, g_other)
    other, other_grads = swapped(other), swapped(other_grads)
    back = exchanged(after(back, back_other, other, other_grads))
    section_out, logit_grad = finish_out(meta, own, own_grads, other, other_grads)
    back_part = swapped(collect_grad(half, meta_other, table, back_other))
    input_grad = collect_grad(half, meta, table, back, back_part)
    return section_out[None], input_grad[None], logit_grad.T[None]


def solution(mesh):
    fine = Mesh(mesh.devices.reshape(SIZES), SECTION + EXPERT)
    placed = (
        P(SECTION, EXPERT, None),
        P(SECTION, EXPERT, None),
        P(SECTION, EXPERT, None),
        P(SECTION, EXPERT, None),
        P(SECTION, None),
        P(SECTION, EXPERT, None, None),
        P(SECTION, EXPERT, None, None),
    )
    return jax.shard_map(
        local,
        mesh=fine,
        in_specs=placed,
        out_specs=(P(SECTION, EXPERT, None),) * 3,
        check_vma=False,
    )
```

```python
import functools

import jax
import jax.numpy as jnp
from jax import lax
from jax.experimental import pallas as pl
from jax.experimental.pallas import tpu as pltpu
from jax.sharding import Mesh, PartitionSpec as P

F32 = jnp.float32
BF16 = jnp.bfloat16
SECTION = ("z_lo", "core")
EXPERT = ("y", "z_hi", "x")
PLANE = ("y", "x")
SIZES = (4, 2, 4, 2, 4)
CAP = 24
VMEM_BYTES = 48 * 1024 * 1024
ANYWHERE = pl.BlockSpec(memory_space=pltpu.VMEM)
SCALAR = pl.BlockSpec(memory_space=pltpu.SMEM)


def dot(a, b, ca, cb):
    return lax.dot_general(a, b, (((ca,), (cb,)), ((), ())), preferred_element_type=F32)


def probabilities(meta):
    raised = jnp.exp(meta[4:8, :])
    return raised / jnp.sum(raised, axis=0, keepdims=True)


def row_marks(meta, table, half, rows):
    copies = table.shape[1]
    tokens = meta.shape[1]
    experts = copies - copies // 8
    ids = meta[0:4, :].astype(jnp.int32)
    label = lax.broadcasted_iota(jnp.int32, (copies, tokens), 0)
    named = [ids[k : k + 1, :] == label for k in range(4)]
    onehot = sum(n.astype(F32) for n in named).astype(BF16)
    earlier = (
        lax.broadcasted_iota(jnp.int32, (tokens, tokens), 0)
        < lax.broadcasted_iota(jnp.int32, (tokens, tokens), 1)
    ).astype(F32).astype(BF16)
    rank = dot(onehot, earlier, 1, 0).astype(jnp.int32)
    copy = lax.broadcasted_iota(jnp.int32, (copies, copies), 1)
    held = table == lax.broadcasted_iota(jnp.int32, (copies, copies), 0)
    first = jnp.sum(jnp.where(held & (copy < experts), copy, 0), axis=1, keepdims=True)
    second = jnp.sum(jnp.where(held & (copy >= experts), copy, 0), axis=1, keepdims=True)
    hot = second > 0
    target = jnp.where(hot & ((rank & 1) == 1), second, first)
    place = jnp.where(hot, rank >> 1, rank)
    row = ((target >> 3) * 4 + (target & 3)) * CAP + place
    row = jnp.where(((target >> 2) & 1) == half, row, -1)
    number = lax.broadcasted_iota(jnp.int32, (rows, tokens), 0)
    return [
        number == jnp.sum(jnp.where(n, row, 0), axis=0, keepdims=True) for n in named
    ]


def either(marks):
    return sum(m.astype(F32) for m in marks)


def weighted(marks, probs):
    return sum(jnp.where(m, probs[k : k + 1, :], 0.0) for k, m in enumerate(marks))


def pack_kernel(half_ref, meta_ref, table_ref, x_ref, g_ref, out_ref):
    meta = meta_ref[...]
    copies = out_ref.shape[0]
    marks = row_marks(meta, table_ref[...], half_ref[0], copies * CAP)
    onehot = either(marks).astype(BF16)
    weight = jnp.sum(weighted(marks, probabilities(meta)), axis=1, keepdims=True)
    x = dot(onehot, x_ref[...], 1, 0)
    g = dot(onehot, g_ref[...], 1, 0) * weight
    for i in range(copies):
        rows = slice(i * CAP, (i + 1) * CAP)
        out_ref[i] = jnp.concatenate([x[rows], g[rows]], axis=0).astype(BF16)


def pack(half, meta, table, x, g):
    width = x.shape[1]
    return pl.pallas_call(
        pack_kernel,
        out_shape=jax.ShapeDtypeStruct((16, 2 * CAP, width), BF16),
        in_specs=[SCALAR] + [ANYWHERE] * 4,
        out_specs=ANYWHERE,
        compiler_params=pltpu.CompilerParams(vmem_limit_bytes=VMEM_BYTES),
        cost_estimate=pl.CostEstimate(
            flops=64 * CAP * x.size, bytes_accessed=4 * x.size + 64 * CAP * width, transcendentals=0
        ),
        name="pack",
    )(half, meta, table, x, g)


def halves(ref):
    both = [ref[i].astype(F32) for i in range(ref.shape[0])]
    first = jnp.concatenate([b[:CAP] for b in both], axis=0).astype(BF16)
    second = jnp.concatenate([b[CAP:] for b in both], axis=0).astype(BF16)
    return first, second


def split_dot(weights, rows):
    high = weights.astype(BF16)
    low = (weights - high.astype(F32)).astype(BF16)
    return dot(high, rows, 0, 0) + dot(low, rows, 0, 0)


def collect_kernel(half_ref, meta_ref, table_ref, rows_ref, g_ref, *refs):
    meta = meta_ref[...]
    out_rows, back_rows = halves(rows_ref)
    marks = row_marks(meta, table_ref[...], half_ref[0], out_rows.shape[0])
    probs = probabilities(meta)
    out = split_dot(weighted(marks, probs), out_rows)
    back = dot(either(marks).astype(BF16), back_rows, 0, 0)
    products = dot(out_rows, g_ref[...], 1, 1)
    grads = jnp.concatenate(
        [jnp.sum(jnp.where(m, products, 0.0), axis=0, keepdims=True) for m in marks], axis=0
    )
    tokens = out.shape[0]
    if len(refs) > 1:
        other_ref, out_ref, back_ref, logit_ref = refs
        out_ref[...] = (out + other_ref[:tokens, :].astype(F32)).astype(BF16)
        back_ref[...] = (back + other_ref[tokens : 2 * tokens, :].astype(F32)).astype(BF16)
        three = other_ref[2 * tokens :, : grads.shape[1]].astype(F32)
        grads = grads + (three[0:4] + three[4:8] + three[8:12])
        logit_ref[...] = probs * (grads - jnp.sum(probs * grads, axis=0, keepdims=True))
    else:
        high = grads.astype(BF16).astype(F32)
        middle = (grads - high).astype(BF16).astype(F32)
        low = grads - high - middle
        three = jnp.concatenate([high, middle, low, jnp.zeros_like(low)], axis=0)
        rest = jnp.zeros((16, out.shape[1] - three.shape[1]), F32)
        refs[0][...] = jnp.concatenate(
            [out, back, jnp.concatenate([three, rest], axis=1)], axis=0
        ).astype(BF16)


def collect(half, meta, table, rows, g, *other):
    tokens, width = g.shape
    whole = jax.ShapeDtypeStruct(g.shape, BF16)
    if other:
        shapes = (whole, whole, jax.ShapeDtypeStruct((4, tokens), F32))
    else:
        shapes = jax.ShapeDtypeStruct((2 * tokens + 16, width), BF16)
    return pl.pallas_call(
        collect_kernel,
        out_shape=shapes,
        in_specs=[SCALAR] + [ANYWHERE] * (4 + len(other)),
        out_specs=(ANYWHERE,) * 3 if other else ANYWHERE,
        compiler_params=pltpu.CompilerParams(vmem_limit_bytes=VMEM_BYTES),
        cost_estimate=pl.CostEstimate(
            flops=4 * rows.size * tokens, bytes_accessed=2 * rows.size + 8 * g.size, transcendentals=0
        ),
        name="collect_last" if other else "collect",
    )(half, meta, table, rows, g, *other)


def expert_kernel(in_ref, wg_ref, wu_ref, wd_ref, out_ref, x_rows, g_rows, out_sum, back_sum):
    step = pl.program_id(0)
    copies = in_ref.shape[0]

    @pl.when(step == 0)
    def _():
        x_rows[...], g_rows[...] = halves(in_ref)

    x = x_rows[...]
    gate = dot(x, wg_ref[...], 1, 0)
    up = dot(x, wu_ref[...], 1, 0)
    hidden_grad = dot(g_rows[...], wd_ref[...], 1, 1)
    sigmoid = jax.nn.sigmoid(gate)
    hidden = (gate * sigmoid * up).astype(BF16)
    gate_grad = (hidden_grad * up * sigmoid * (1.0 + gate * (1.0 - sigmoid))).astype(BF16)
    up_grad = (hidden_grad * gate * sigmoid).astype(BF16)
    out = dot(hidden, wd_ref[...], 1, 0)
    back = dot(gate_grad, wg_ref[...], 1, 1) + dot(up_grad, wu_ref[...], 1, 1)

    @pl.when(step == 0)
    def _():
        out_sum[...] = out
        back_sum[...] = back

    @pl.when(step > 0)
    def _():
        out_sum[...] += out
        back_sum[...] += back

    @pl.when(step == pl.num_programs(0) - 1)
    def _():
        for i in range(copies):
            rows = slice(i * CAP, (i + 1) * CAP)
            out_ref[i] = jnp.concatenate([out_sum[rows, :], back_sum[rows, :]], axis=0).astype(BF16)


BLOCK = 256


def expert(both, w_gu, w_dn):
    copies, _, width = both.shape
    hidden = w_dn.shape[0]
    steps = hidden // BLOCK
    rows = copies * CAP
    return pl.pallas_call(
        expert_kernel,
        grid=(steps,),
        out_shape=jax.ShapeDtypeStruct(both.shape, BF16),
        in_specs=[
            pl.BlockSpec(both.shape, lambda j: (0, 0, 0)),
            pl.BlockSpec((width, BLOCK), lambda j: (0, j)),
            pl.BlockSpec((width, BLOCK), lambda j: (0, steps + j)),
            pl.BlockSpec((BLOCK, width), lambda j: (j, 0)),
        ],
        out_specs=pl.BlockSpec(both.shape, lambda j: (0, 0, 0)),
        scratch_shapes=[pltpu.VMEM((rows, width), BF16)] * 2 + [pltpu.VMEM((rows, width), F32)] * 2,
        compiler_params=pltpu.CompilerParams(vmem_limit_bytes=VMEM_BYTES),
        cost_estimate=pl.CostEstimate(
            flops=12 * rows * width * hidden,
            bytes_accessed=6 * width * hidden + 8 * rows * width,
            transcendentals=rows * hidden,
        ),
        name="expert",
    )(both, w_gu, w_gu, w_dn)


def after(x, *earlier):
    return lax.optimization_barrier((x, *earlier))[0]


def shifted(x, by):
    sections = SIZES[0] * SIZES[1]
    pairs = [(i, i + by) for i in range(sections) if 0 <= i + by < sections]
    here = lax.axis_index(SECTION) == (0 if by > 0 else sections - 1)
    return jnp.where(here, x, lax.ppermute(x, SECTION, pairs))


def swapped(x, cores=(0, 1)):
    pairs = [(2 * c + h, 2 * c + 1 - h) for c in cores for h in range(2)]
    return lax.ppermute(x, ("core", "z_hi"), pairs)


def exchanged(rows):
    return lax.all_to_all(rows, PLANE, split_axis=0, concat_axis=0, tiled=True)


def local(x_held, grad_held, expert_ids, gate_logits, placement, w_gate_up, w_down):
    w_gu = w_gate_up[0, 0]
    w_dn = w_down[0, 0]
    half = lax.axis_index("z_hi").astype(jnp.int32).reshape(1)
    table = placement
    odd = lax.axis_index("core") == 1

    meta = jnp.concatenate([expert_ids[0].astype(F32).T, gate_logits[0].T], axis=0)
    meta_other = swapped(meta)
    x = shifted(x_held[0], 1)
    g = shifted(grad_held[0], -1)
    x_odd = lax.ppermute(
        x_held[0],
        SECTION + ("z_hi",),
        [(4 * i + h, 4 * i + 3 - h) for i in range(SIZES[0]) for h in range(2)],
    )
    x_even = swapped(after(x, g), (0,))
    packed = after(pack(half, meta, table, x, g), x_even, x_odd)
    rows = exchanged(packed)
    g_other = swapped(after(g, packed))
    x_other = jnp.where(odd, x_odd, x_even)
    rows_other = exchanged(after(pack(half, meta_other, table, x_other, g_other), rows))

    done = expert(rows, w_gu, w_dn)
    done_other = exchanged(expert(rows_other, w_gu, w_dn))
    part = swapped(collect(half, meta_other, table, done_other, g_other))
    done = exchanged(after(done, done_other))
    section_out, input_grad, logit_grad = collect(half, meta, table, done, g, part)
    return section_out[None], input_grad[None], logit_grad.T[None]


def solution(mesh):
    fine = Mesh(mesh.devices.reshape(SIZES), SECTION + EXPERT)
    placed = (
        P(SECTION, EXPERT, None),
        P(SECTION, EXPERT, None),
        P(SECTION, EXPERT, None),
        P(SECTION, EXPERT, None),
        P(SECTION, None),
        P(SECTION, EXPERT, None, None),
        P(SECTION, EXPERT, None, None),
    )
    return jax.shard_map(
        local,
        mesh=fine,
        in_specs=placed,
        out_specs=(P(SECTION, EXPERT, None),) * 3,
        check_vma=False,
    )
```

```python
import functools

import jax
import jax.numpy as jnp
from jax import lax
from jax.experimental import pallas as pl
from jax.experimental.pallas import tpu as pltpu
from jax.sharding import Mesh, PartitionSpec as P

F32 = jnp.float32
BF16 = jnp.bfloat16
SECTION = ("z_lo", "core")
EXPERT = ("y", "z_hi", "x")
PLANE = ("y", "x")
SIZES = (4, 2, 4, 2, 4)
CAP = 24
VMEM_BYTES = 28 * 1024 * 1024
EXPERT_BYTES = 40 * 1024 * 1024
ANYWHERE = pl.BlockSpec(memory_space=pltpu.VMEM)
SCALAR = pl.BlockSpec(memory_space=pltpu.SMEM)


def dot(a, b, ca, cb):
    return lax.dot_general(a, b, (((ca,), (cb,)), ((), ())), preferred_element_type=F32)


def probabilities(meta):
    raised = jnp.exp(meta[4:8, :])
    return raised / jnp.sum(raised, axis=0, keepdims=True)


def row_marks(meta, table, half, rows):
    copies = table.shape[1]
    tokens = meta.shape[1]
    experts = copies - copies // 8
    ids = meta[0:4, :].astype(jnp.int32)
    label = lax.broadcasted_iota(jnp.int32, (copies, tokens), 0)
    named = [ids[k : k + 1, :] == label for k in range(4)]
    onehot = sum(n.astype(F32) for n in named).astype(BF16)
    earlier = (
        lax.broadcasted_iota(jnp.int32, (tokens, tokens), 0)
        < lax.broadcasted_iota(jnp.int32, (tokens, tokens), 1)
    ).astype(F32).astype(BF16)
    rank = dot(onehot, earlier, 1, 0).astype(jnp.int32)
    copy = lax.broadcasted_iota(jnp.int32, (copies, copies), 1)
    held = table == lax.broadcasted_iota(jnp.int32, (copies, copies), 0)
    first = jnp.sum(jnp.where(held & (copy < experts), copy, 0), axis=1, keepdims=True)
    second = jnp.sum(jnp.where(held & (copy >= experts), copy, 0), axis=1, keepdims=True)
    hot = second > 0
    target = jnp.where(hot & ((rank & 1) == 1), second, first)
    place = jnp.where(hot, rank >> 1, rank)
    row = ((target >> 3) * 4 + (target & 3)) * CAP + place
    row = jnp.where(((target >> 2) & 1) == half, row, -1)
    number = lax.broadcasted_iota(jnp.int32, (rows, tokens), 0)
    return [
        number == jnp.sum(jnp.where(n, row, 0), axis=0, keepdims=True) for n in named
    ]


def either(marks):
    return sum(m.astype(F32) for m in marks)


def weighted(marks, probs):
    return sum(jnp.where(m, probs[k : k + 1, :], 0.0) for k, m in enumerate(marks))


def pack_kernel(half_ref, meta_ref, table_ref, x_ref, g_ref, out_ref):
    meta = meta_ref[...]
    copies = out_ref.shape[0]
    marks = row_marks(meta, table_ref[...], half_ref[0], copies * CAP)
    onehot = either(marks).astype(BF16)
    weight = jnp.sum(weighted(marks, probabilities(meta)), axis=1, keepdims=True)
    x = dot(onehot, x_ref[...], 1, 0)
    g = dot(onehot, g_ref[...], 1, 0) * weight
    for i in range(copies):
        rows = slice(i * CAP, (i + 1) * CAP)
        out_ref[i] = jnp.concatenate([x[rows], g[rows]], axis=0).astype(BF16)


def pack(half, meta, table, x, g):
    width = x.shape[1]
    return pl.pallas_call(
        pack_kernel,
        out_shape=jax.ShapeDtypeStruct((16, 2 * CAP, width), BF16),
        in_specs=[SCALAR] + [ANYWHERE] * 4,
        out_specs=ANYWHERE,
        compiler_params=pltpu.CompilerParams(vmem_limit_bytes=VMEM_BYTES),
        cost_estimate=pl.CostEstimate(
            flops=64 * CAP * x.size, bytes_accessed=4 * x.size + 64 * CAP * width, transcendentals=0
        ),
        name="pack",
    )(half, meta, table, x, g)


def halves(ref):
    both = [ref[i].astype(F32) for i in range(ref.shape[0])]
    first = jnp.concatenate([b[:CAP] for b in both], axis=0).astype(BF16)
    second = jnp.concatenate([b[CAP:] for b in both], axis=0).astype(BF16)
    return first, second


def split_dot(weights, rows):
    high = weights.astype(BF16)
    low = (weights - high.astype(F32)).astype(BF16)
    return dot(high, rows, 0, 0) + dot(low, rows, 0, 0)


def collect_kernel(half_ref, meta_ref, table_ref, rows_ref, g_ref, *refs):
    meta = meta_ref[...]
    out_rows, back_rows = halves(rows_ref)
    marks = row_marks(meta, table_ref[...], half_ref[0], out_rows.shape[0])
    probs = probabilities(meta)
    out = split_dot(weighted(marks, probs), out_rows)
    back = dot(either(marks).astype(BF16), back_rows, 0, 0)
    products = dot(out_rows, g_ref[...], 1, 1)
    grads = jnp.concatenate(
        [jnp.sum(jnp.where(m, products, 0.0), axis=0, keepdims=True) for m in marks], axis=0
    )
    tokens = out.shape[0]
    if len(refs) > 1:
        other_ref, out_ref, back_ref, logit_ref = refs
        out_ref[...] = (out + other_ref[:tokens, :].astype(F32)).astype(BF16)
        back_ref[...] = (back + other_ref[tokens : 2 * tokens, :].astype(F32)).astype(BF16)
        three = other_ref[2 * tokens :, : grads.shape[1]].astype(F32)
        grads = grads + (three[0:4] + three[4:8] + three[8:12])
        logit_ref[...] = probs * (grads - jnp.sum(probs * grads, axis=0, keepdims=True))
    else:
        high = grads.astype(BF16).astype(F32)
        middle = (grads - high).astype(BF16).astype(F32)
        low = grads - high - middle
        three = jnp.concatenate([high, middle, low, jnp.zeros_like(low)], axis=0)
        rest = jnp.zeros((16, out.shape[1] - three.shape[1]), F32)
        refs[0][...] = jnp.concatenate(
            [out, back, jnp.concatenate([three, rest], axis=1)], axis=0
        ).astype(BF16)


def collect(half, meta, table, rows, g, *other):
    tokens, width = g.shape
    whole = jax.ShapeDtypeStruct(g.shape, BF16)
    if other:
        shapes = (whole, whole, jax.ShapeDtypeStruct((4, tokens), F32))
    else:
        shapes = jax.ShapeDtypeStruct((2 * tokens + 16, width), BF16)
    return pl.pallas_call(
        collect_kernel,
        out_shape=shapes,
        in_specs=[SCALAR] + [ANYWHERE] * (4 + len(other)),
        out_specs=(ANYWHERE,) * 3 if other else ANYWHERE,
        compiler_params=pltpu.CompilerParams(vmem_limit_bytes=VMEM_BYTES),
        cost_estimate=pl.CostEstimate(
            flops=4 * rows.size * tokens, bytes_accessed=2 * rows.size + 8 * g.size, transcendentals=0
        ),
        name="collect_last" if other else "collect",
    )(half, meta, table, rows, g, *other)


def expert_kernel(in_ref, wg_ref, wu_ref, wd_ref, out_ref, x_rows, g_rows, out_sum, back_sum):
    step = pl.program_id(0)
    copies = in_ref.shape[0]

    @pl.when(step == 0)
    def _():
        x_rows[...], g_rows[...] = halves(in_ref)

    x = x_rows[...]
    gate = dot(x, wg_ref[...], 1, 0)
    up = dot(x, wu_ref[...], 1, 0)
    hidden_grad = dot(g_rows[...], wd_ref[...], 1, 1)
    sigmoid = jax.nn.sigmoid(gate)
    hidden = (gate * sigmoid * up).astype(BF16)
    gate_grad = (hidden_grad * up * sigmoid * (1.0 + gate * (1.0 - sigmoid))).astype(BF16)
    up_grad = (hidden_grad * gate * sigmoid).astype(BF16)
    out = dot(hidden, wd_ref[...], 1, 0)
    back = dot(gate_grad, wg_ref[...], 1, 1) + dot(up_grad, wu_ref[...], 1, 1)

    @pl.when(step == 0)
    def _():
        out_sum[...] = out
        back_sum[...] = back

    @pl.when(step > 0)
    def _():
        out_sum[...] += out
        back_sum[...] += back

    @pl.when(step == pl.num_programs(0) - 1)
    def _():
        for i in range(copies):
            rows = slice(i * CAP, (i + 1) * CAP)
            out_ref[i] = jnp.concatenate([out_sum[rows, :], back_sum[rows, :]], axis=0).astype(BF16)


BLOCK = 256


def expert(both, w_gu, w_dn):
    copies, _, width = both.shape
    hidden = w_dn.shape[0]
    steps = hidden // BLOCK
    rows = copies * CAP
    return pl.pallas_call(
        expert_kernel,
        grid=(steps,),
        out_shape=jax.ShapeDtypeStruct(both.shape, BF16),
        in_specs=[
            pl.BlockSpec(both.shape, lambda j: (0, 0, 0)),
            pl.BlockSpec((width, BLOCK), lambda j: (0, j)),
            pl.BlockSpec((width, BLOCK), lambda j: (0, steps + j)),
            pl.BlockSpec((BLOCK, width), lambda j: (j, 0)),
        ],
        out_specs=pl.BlockSpec(both.shape, lambda j: (0, 0, 0)),
        scratch_shapes=[pltpu.VMEM((rows, width), BF16)] * 2 + [pltpu.VMEM((rows, width), F32)] * 2,
        compiler_params=pltpu.CompilerParams(vmem_limit_bytes=EXPERT_BYTES),
        cost_estimate=pl.CostEstimate(
            flops=12 * rows * width * hidden,
            bytes_accessed=6 * width * hidden + 8 * rows * width,
            transcendentals=rows * hidden,
        ),
        name="expert",
    )(both, w_gu, w_gu, w_dn)


def after(x, *earlier):
    return lax.optimization_barrier((x, *earlier))[0]


def shifted(x, by):
    sections = SIZES[0] * SIZES[1]
    pairs = [(i, i + by) for i in range(sections) if 0 <= i + by < sections]
    here = lax.axis_index(SECTION) == (0 if by > 0 else sections - 1)
    return jnp.where(here, x, lax.ppermute(x, SECTION, pairs))


def swapped(x, cores=(0, 1)):
    pairs = [(2 * c + h, 2 * c + 1 - h) for c in cores for h in range(2)]
    return lax.ppermute(x, ("core", "z_hi"), pairs)


def exchanged(rows):
    return lax.all_to_all(rows, PLANE, split_axis=0, concat_axis=0, tiled=True)


def local(x_held, grad_held, expert_ids, gate_logits, placement, w_gate_up, w_down):
    w_gu = w_gate_up[0, 0]
    w_dn = w_down[0, 0]
    half = lax.axis_index("z_hi").astype(jnp.int32).reshape(1)
    table = placement
    odd = lax.axis_index("core") == 1

    meta = jnp.concatenate([expert_ids[0].astype(F32).T, gate_logits[0].T], axis=0)
    meta_other = swapped(meta)
    x = shifted(x_held[0], 1)
    g = shifted(grad_held[0], -1)
    x_odd = lax.ppermute(
        x_held[0],
        SECTION + ("z_hi",),
        [(4 * i + h, 4 * i + 3 - h) for i in range(SIZES[0]) for h in range(2)],
    )
    x_even = swapped(after(x, g, x_odd), (0,))
    packed = after(pack(half, meta, table, x, g), x_even, x_odd)
    rows = exchanged(packed)
    g_other = swapped(after(g, packed))
    x_other = jnp.where(odd, x_odd, x_even)
    rows_other = exchanged(after(pack(half, meta_other, table, x_other, g_other), rows))

    done = expert(rows, w_gu, w_dn)
    done_other = exchanged(expert(rows_other, w_gu, w_dn))
    part = swapped(collect(half, meta_other, table, done_other, g_other))
    done = exchanged(after(done, done_other))
    section_out, input_grad, logit_grad = collect(half, meta, table, done, g, part)
    return section_out[None], input_grad[None], logit_grad.T[None]


def solution(mesh):
    fine = Mesh(mesh.devices.reshape(SIZES), SECTION + EXPERT)
    placed = (
        P(SECTION, EXPERT, None),
        P(SECTION, EXPERT, None),
        P(SECTION, EXPERT, None),
        P(SECTION, EXPERT, None),
        P(SECTION, None),
        P(SECTION, EXPERT, None, None),
        P(SECTION, EXPERT, None, None),
    )
    return jax.shard_map(
        local,
        mesh=fine,
        in_specs=placed,
        out_specs=(P(SECTION, EXPERT, None),) * 3,
        check_vma=False,
    )
```

```python
import functools

import jax
import jax.numpy as jnp
from jax import lax
from jax.experimental import pallas as pl
from jax.experimental.pallas import tpu as pltpu
from jax.sharding import Mesh, PartitionSpec as P

F32 = jnp.float32
BF16 = jnp.bfloat16
SECTION = ("z_lo", "core")
EXPERT = ("y", "z_hi", "x")
PLANE = ("y", "x")
SIZES = (4, 2, 4, 2, 4)
CAP = 24
VMEM_BYTES = 28 * 1024 * 1024
EXPERT_BYTES = 40 * 1024 * 1024
ANYWHERE = pl.BlockSpec(memory_space=pltpu.VMEM)
SCALAR = pl.BlockSpec(memory_space=pltpu.SMEM)


def dot(a, b, ca, cb):
    return lax.dot_general(a, b, (((ca,), (cb,)), ((), ())), preferred_element_type=F32)


def probabilities(meta):
    raised = jnp.exp(meta[4:8, :])
    return raised / jnp.sum(raised, axis=0, keepdims=True)


def row_marks(meta, table, half, rows):
    copies = table.shape[1]
    tokens = meta.shape[1]
    experts = copies - copies // 8
    ids = meta[0:4, :].astype(jnp.int32)
    label = lax.broadcasted_iota(jnp.int32, (copies, tokens), 0)
    named = [ids[k : k + 1, :] == label for k in range(4)]
    onehot = sum(n.astype(F32) for n in named).astype(BF16)
    earlier = (
        lax.broadcasted_iota(jnp.int32, (tokens, tokens), 0)
        < lax.broadcasted_iota(jnp.int32, (tokens, tokens), 1)
    ).astype(F32).astype(BF16)
    rank = dot(onehot, earlier, 1, 0).astype(jnp.int32)
    copy = lax.broadcasted_iota(jnp.int32, (copies, copies), 1)
    held = table == lax.broadcasted_iota(jnp.int32, (copies, copies), 0)
    first = jnp.sum(jnp.where(held & (copy < experts), copy, 0), axis=1, keepdims=True)
    second = jnp.sum(jnp.where(held & (copy >= experts), copy, 0), axis=1, keepdims=True)
    hot = second > 0
    target = jnp.where(hot & ((rank & 1) == 1), second, first)
    place = jnp.where(hot, rank >> 1, rank)
    row = ((target >> 3) * 4 + (target & 3)) * CAP + place
    row = jnp.where(((target >> 2) & 1) == half, row, -1)
    number = lax.broadcasted_iota(jnp.int32, (rows, tokens), 0)
    return [
        number == jnp.sum(jnp.where(n, row, 0), axis=0, keepdims=True) for n in named
    ]


def either(marks):
    return sum(m.astype(F32) for m in marks)


def weighted(marks, probs):
    return sum(jnp.where(m, probs[k : k + 1, :], 0.0) for k, m in enumerate(marks))


def pack_kernel(half_ref, meta_ref, table_ref, x_ref, g_ref, out_ref):
    meta = meta_ref[...]
    copies = out_ref.shape[0]
    marks = row_marks(meta, table_ref[...], half_ref[0], copies * CAP)
    onehot = either(marks).astype(BF16)
    weight = jnp.sum(weighted(marks, probabilities(meta)), axis=1, keepdims=True)
    x = dot(onehot, x_ref[...], 1, 0)
    g = dot(onehot, g_ref[...], 1, 0) * weight
    for i in range(copies):
        rows = slice(i * CAP, (i + 1) * CAP)
        out_ref[i] = jnp.concatenate([x[rows], g[rows]], axis=0).astype(BF16)


def pack(half, meta, table, x, g):
    width = x.shape[1]
    return pl.pallas_call(
        pack_kernel,
        out_shape=jax.ShapeDtypeStruct((16, 2 * CAP, width), BF16),
        in_specs=[SCALAR] + [ANYWHERE] * 4,
        out_specs=ANYWHERE,
        compiler_params=pltpu.CompilerParams(vmem_limit_bytes=VMEM_BYTES),
        cost_estimate=pl.CostEstimate(
            flops=64 * CAP * x.size, bytes_accessed=4 * x.size + 64 * CAP * width, transcendentals=0
        ),
        name="pack",
    )(half, meta, table, x, g)


def halves(ref):
    both = [ref[i].astype(F32) for i in range(ref.shape[0])]
    first = jnp.concatenate([b[:CAP] for b in both], axis=0).astype(BF16)
    second = jnp.concatenate([b[CAP:] for b in both], axis=0).astype(BF16)
    return first, second


def split_dot(weights, rows):
    high = weights.astype(BF16)
    low = (weights - high.astype(F32)).astype(BF16)
    return dot(high, rows, 0, 0) + dot(low, rows, 0, 0)


def collect_kernel(half_ref, meta_ref, table_ref, rows_ref, g_ref, *refs):
    meta = meta_ref[...]
    out_rows, back_rows = halves(rows_ref)
    marks = row_marks(meta, table_ref[...], half_ref[0], out_rows.shape[0])
    probs = probabilities(meta)
    out = split_dot(weighted(marks, probs), out_rows)
    back = dot(either(marks).astype(BF16), back_rows, 0, 0)
    products = dot(out_rows, g_ref[...], 1, 1)
    grads = jnp.concatenate(
        [jnp.sum(jnp.where(m, products, 0.0), axis=0, keepdims=True) for m in marks], axis=0
    )
    tokens = out.shape[0]
    if len(refs) > 1:
        other_ref, out_ref, back_ref, logit_ref = refs
        out_ref[...] = (out + other_ref[:tokens, :].astype(F32)).astype(BF16)
        back_ref[...] = (back + other_ref[tokens : 2 * tokens, :].astype(F32)).astype(BF16)
        three = other_ref[2 * tokens :, : grads.shape[1]].astype(F32)
        grads = grads + (three[0:4] + three[4:8] + three[8:12])
        logit_ref[...] = probs * (grads - jnp.sum(probs * grads, axis=0, keepdims=True))
    else:
        high = grads.astype(BF16).astype(F32)
        middle = (grads - high).astype(BF16).astype(F32)
        low = grads - high - middle
        three = jnp.concatenate([high, middle, low, jnp.zeros_like(low)], axis=0)
        rest = jnp.zeros((16, out.shape[1] - three.shape[1]), F32)
        refs[0][...] = jnp.concatenate(
            [out, back, jnp.concatenate([three, rest], axis=1)], axis=0
        ).astype(BF16)


def collect(half, meta, table, rows, g, *other):
    tokens, width = g.shape
    whole = jax.ShapeDtypeStruct(g.shape, BF16)
    if other:
        shapes = (whole, whole, jax.ShapeDtypeStruct((4, tokens), F32))
    else:
        shapes = jax.ShapeDtypeStruct((2 * tokens + 16, width), BF16)
    return pl.pallas_call(
        collect_kernel,
        out_shape=shapes,
        in_specs=[SCALAR] + [ANYWHERE] * (4 + len(other)),
        out_specs=(ANYWHERE,) * 3 if other else ANYWHERE,
        compiler_params=pltpu.CompilerParams(vmem_limit_bytes=VMEM_BYTES),
        cost_estimate=pl.CostEstimate(
            flops=4 * rows.size * tokens, bytes_accessed=2 * rows.size + 8 * g.size, transcendentals=0
        ),
        name="collect_last" if other else "collect",
    )(half, meta, table, rows, g, *other)


def expert_kernel(in_ref, wg_ref, wu_ref, wd_ref, out_ref, x_rows, g_rows, out_sum, back_sum):
    step = pl.program_id(0)
    copies = in_ref.shape[0]

    @pl.when(step == 0)
    def _():
        x_rows[...], g_rows[...] = halves(in_ref)

    x = x_rows[...]
    gate = dot(x, wg_ref[...], 1, 0)
    up = dot(x, wu_ref[...], 1, 0)
    hidden_grad = dot(g_rows[...], wd_ref[...], 1, 1)
    sigmoid = jax.nn.sigmoid(gate)
    silu = gate * sigmoid
    hidden = (silu * up).astype(BF16)
    gate_grad = (hidden_grad * up * (sigmoid + silu * (1.0 - sigmoid))).astype(BF16)
    up_grad = (hidden_grad * silu).astype(BF16)
    out = dot(hidden, wd_ref[...], 1, 0)
    back = dot(gate_grad, wg_ref[...], 1, 1) + dot(up_grad, wu_ref[...], 1, 1)

    @pl.when(step == 0)
    def _():
        out_sum[...] = out
        back_sum[...] = back

    @pl.when(step > 0)
    def _():
        out_sum[...] += out
        back_sum[...] += back

    @pl.when(step == pl.num_programs(0) - 1)
    def _():
        for i in range(copies):
            rows = slice(i * CAP, (i + 1) * CAP)
            out_ref[i] = jnp.concatenate([out_sum[rows, :], back_sum[rows, :]], axis=0).astype(BF16)


BLOCK = 256


def expert(both, w_gu, w_dn):
    copies, _, width = both.shape
    hidden = w_dn.shape[0]
    steps = hidden // BLOCK
    rows = copies * CAP
    return pl.pallas_call(
        expert_kernel,
        grid=(steps,),
        out_shape=jax.ShapeDtypeStruct(both.shape, BF16),
        in_specs=[
            pl.BlockSpec(both.shape, lambda j: (0, 0, 0)),
            pl.BlockSpec((width, BLOCK), lambda j: (0, j)),
            pl.BlockSpec((width, BLOCK), lambda j: (0, steps + j)),
            pl.BlockSpec((BLOCK, width), lambda j: (j, 0)),
        ],
        out_specs=pl.BlockSpec(both.shape, lambda j: (0, 0, 0)),
        scratch_shapes=[pltpu.VMEM((rows, width), BF16)] * 2 + [pltpu.VMEM((rows, width), F32)] * 2,
        compiler_params=pltpu.CompilerParams(vmem_limit_bytes=EXPERT_BYTES),
        cost_estimate=pl.CostEstimate(
            flops=12 * rows * width * hidden,
            bytes_accessed=6 * width * hidden + 8 * rows * width,
            transcendentals=rows * hidden,
        ),
        name="expert",
    )(both, w_gu, w_gu, w_dn)


def after(x, *earlier):
    return lax.optimization_barrier((x, *earlier))[0]


def shifted(x, by):
    sections = SIZES[0] * SIZES[1]
    pairs = [(i, i + by) for i in range(sections) if 0 <= i + by < sections]
    here = lax.axis_index(SECTION) == (0 if by > 0 else sections - 1)
    return jnp.where(here, x, lax.ppermute(x, SECTION, pairs))


def swapped(x, cores=(0, 1)):
    pairs = [(2 * c + h, 2 * c + 1 - h) for c in cores for h in range(2)]
    return lax.ppermute(x, ("core", "z_hi"), pairs)


def exchanged(rows):
    return lax.all_to_all(rows, PLANE, split_axis=0, concat_axis=0, tiled=True)


def local(x_held, grad_held, expert_ids, gate_logits, placement, w_gate_up, w_down):
    w_gu = w_gate_up[0, 0]
    w_dn = w_down[0, 0]
    half = lax.axis_index("z_hi").astype(jnp.int32).reshape(1)
    table = placement
    odd = lax.axis_index("core") == 1

    meta = jnp.concatenate([expert_ids[0].astype(F32).T, gate_logits[0].T], axis=0)
    meta_other = swapped(meta)
    x = shifted(x_held[0], 1)
    g = shifted(grad_held[0], -1)
    x_odd = lax.ppermute(
        x_held[0],
        SECTION + ("z_hi",),
        [(4 * i + h, 4 * i + 3 - h) for i in range(SIZES[0]) for h in range(2)],
    )
    x_even = swapped(after(x, g, x_odd), (0,))
    packed = after(pack(half, meta, table, x, g), x_even, x_odd)
    rows = exchanged(packed)
    g_other = swapped(after(g, packed))
    x_other = jnp.where(odd, x_odd, x_even)
    rows_other = exchanged(after(pack(half, meta_other, table, x_other, g_other), rows))

    done = expert(rows, w_gu, w_dn)
    done_other = exchanged(expert(rows_other, w_gu, w_dn))
    part = swapped(collect(half, meta_other, table, done_other, g_other))
    done = exchanged(after(done, done_other))
    section_out, input_grad, logit_grad = collect(half, meta, table, done, g, part)
    return section_out[None], input_grad[None], logit_grad.T[None]


def solution(mesh):
    fine = Mesh(mesh.devices.reshape(SIZES), SECTION + EXPERT)
    placed = (
        P(SECTION, EXPERT, None),
        P(SECTION, EXPERT, None),
        P(SECTION, EXPERT, None),
        P(SECTION, EXPERT, None),
        P(SECTION, None),
        P(SECTION, EXPERT, None, None),
        P(SECTION, EXPERT, None, None),
    )
    return jax.shard_map(
        local,
        mesh=fine,
        in_specs=placed,
        out_specs=(P(SECTION, EXPERT, None),) * 3,
        check_vma=False,
    )
```
